128 devices in a mesh: group: 16 (over y, x), member: 8 (over z, core).
Axes of the slice: x: 4, y: 4, z: 4, core: 2. Of those that a mesh axis runs over, the one named last changes fastest.
Arguments:
- embeddings: bfloat16 [524288, 256], P(('group', 'member')), may hold values from -64 to 64
- cluster_ids: int32 [524288], P(('group', 'member')), may hold values from 0 to 15, as said below
- centroids: bfloat16 [16, 4096, 256], P('group', 'member'), may hold values from -40 to 40
Outputs:
- new_centroids: float32 [16, 4096, 256], P('group', 'member')
- mass: float32 [16, 4096], P('group', 'member')
The draws below stay inside these ranges and needn't reach their ends.
Inputs may be any that keep to these rules, and one draw needn't show every extreme that they name: `cluster_ids`: each device's 4096 rows hold exactly 256 rows of every cluster.
All inputs are finite; a program needn't handle non-finite values.
Results may differ from the reference program's by a relative error of at most 0.0006.
Values may be sent and summed in bfloat16 or wider, within the bound.
A program may use at most 64 MiB of HBM per device.

```python
import math
import jax
import jax.numpy as jnp
from jax import lax

D = 256
K_SUB = 4096
ROW_DEV = 4096
CLUSTERS = 16
ROWS = 524288


def cluster_table(key):
    device_count = ROWS // ROW_DEV
    keys = jax.random.split(jax.random.fold_in(key, 7), device_count)
    perms = jax.vmap(lambda one_key: jax.random.permutation(one_key, ROW_DEV))(keys)
    return (perms % CLUSTERS).reshape(-1).astype(jnp.int32)


def centre_table(key):
    base = jax.random.normal(jax.random.fold_in(key, 11), (CLUSTERS, K_SUB, D), jnp.float32)
    return jnp.clip(base, -6.0, 6.0)


def draw_cluster_ids(key, part):
    return cluster_table(key)


def draw_centroids(key, part):
    return centre_table(key).astype(jnp.bfloat16)


def draw_embeddings(key, part):
    base = jax.random.normal(jax.random.fold_in(key, 21), (ROWS, D), jnp.float32)
    return jnp.clip(base, -6.0, 6.0).astype(jnp.bfloat16)


def setup_inputs(seed: int = 0) -> dict:
    key_list = jax.random.split(jax.random.key(seed), 4)
    embeddings = draw_embeddings(jax.random.fold_in(key_list[3], 71), 0)
    cluster_ids = draw_cluster_ids(jax.random.fold_in(key_list[3], 71), 0)
    centroids = draw_centroids(jax.random.fold_in(key_list[3], 71), 0)
    return dict(embeddings=embeddings, cluster_ids=cluster_ids, centroids=centroids)


PRIOR_MASS = 1.0

def reference(embeddings, cluster_ids, centroids):
    row_order = jnp.argsort(cluster_ids, stable=True)
    grouped = embeddings[row_order].reshape(CLUSTERS, -1, D)
    norms = lax.optimization_barrier(jnp.sum(jnp.square(centroids.astype(jnp.float32)), axis=-1))
    factor = 2.0 / math.sqrt(D)

    def one_cluster(packed):
        cluster_rows, centres, centre_norms = packed
        row_total = cluster_rows.shape[0]
        block_rows = min(512, row_total)
        blocks = cluster_rows.reshape(row_total // block_rows, block_rows, D)

        def visit(carry, block_x):
            weighted, total_mass = carry
            scores = lax.dot_general(block_x, centres, (((1,), (1,)), ((), ())), preferred_element_type=jnp.float32)
            logits = (scores - 0.5 * centre_norms) * factor
            weights_block = jax.nn.softmax(logits, axis=-1).astype(jnp.bfloat16)
            weighted = weighted + lax.dot_general(weights_block, block_x, (((0,), (0,)), ((), ())), preferred_element_type=jnp.float32)
            total_mass = total_mass + lax.optimization_barrier(jnp.sum(weights_block.astype(jnp.float32), axis=0))
            return ((weighted, total_mass), None)
        start = (jnp.zeros((K_SUB, D), jnp.float32), jnp.zeros((K_SUB,), jnp.float32))
        (weighted, total_mass), _ = lax.scan(visit, start, blocks)
        updated = (weighted + PRIOR_MASS * centres.astype(jnp.float32)) / (total_mass + PRIOR_MASS)[:, None]
        return (updated, total_mass)
    new_centroids, mass = lax.map(one_cluster, (grouped, centroids, norms))
    return (new_centroids, mass)
```

```python
import functools
import math

import jax
import jax.numpy as jnp
from jax import lax
from jax.experimental import pallas as pl
from jax.experimental.pallas import tpu as pltpu
from jax.sharding import PartitionSpec as P

F32, BF16 = jnp.float32, jnp.bfloat16
MESH = pl.DeviceIdType.MESH
NT = (((1,), (1,)), ((), ()))
LOG2E = 1.4426950408889634
PRIOR_MASS = 1.0

SIDE = 4
CLUSTERS = 16
D = 256
ROWS = 4096
BLOCK = 256
BLOCKS = 32
CHUNK = 256
CHUNKS = 8
OWN = 512
WROWS = 264


def iota(shape, dim):
    return lax.broadcasted_iota(jnp.int32, shape, dim)


def ranks(ids, r_ref):
    upper = (iota((128, 128), 0) <= iota((128, 128), 1)).astype(F32).astype(BF16)
    ones = jnp.ones((128, 128), BF16)
    ri, ci = iota((128, 128), 0), iota((128, 128), 1)
    before = ((ri // 32 == ci // 32) & (ci < ri)).astype(F32).astype(BF16)
    for quad in range(CLUSTERS // 4):
        eq = jnp.concatenate(
            [(ids == quad * 4 + i).astype(F32) for i in range(4)], axis=0
        )
        hot = eq.astype(BF16)
        inside = jnp.dot(hot, upper, preferred_element_type=F32)
        totals = jnp.dot(hot, ones, preferred_element_type=F32).astype(BF16)
        ahead = jnp.dot(before, totals, preferred_element_type=F32)
        rank = jnp.where(eq > 0.5, inside + ahead - 1.0, -1.0)
        for i in range(4):
            r_ref[quad * 4 + i] = rank[i * 32 : (i + 1) * 32]


def permuted(cluster, r_ref, embt_ref):
    rank = r_ref[cluster]
    place = iota((BLOCK, 128), 0).astype(F32).astype(BF16)
    acc = None
    for chunk in range(8):
        hots = []
        for t in range(chunk * 4, chunk * 4 + 4):
            row = jnp.broadcast_to(rank[t : t + 1], (BLOCK, 128)).astype(BF16)
            hots.append(jnp.where(row == place, jnp.ones_like(place), jnp.zeros_like(place)))
        hot = jnp.concatenate(hots, axis=1)
        part = lax.dot_general(
            embt_ref[:, chunk * 512 : (chunk + 1) * 512], hot, NT, preferred_element_type=F32
        )
        acc = part if acc is None else acc + part
    return acc.astype(BF16)


def kernel(emb_ref, ids_ref, cent_ref, out_ref, mass_ref,
           embt_ref, send_ref, xt_ref, r_ref, cbuf_ref, bias_ref, e_ref,
           m_ref, s_ref, stat_ref, peer_ref, f_ref, acc_ref, rs_ref, rr_ref,
           row_s, row_r, cent_s, cent_r, fwd_s, fwd_r, stat_s, stat_r, ring_s, ring_r):
    g, m = lax.axis_index("group"), lax.axis_index("member")
    y, x = g // SIDE, g % SIDE
    z, core = m // 2, m % 2
    partner = (g, z * 2 + 1 - core)

    def plane(o):
        return ((y + o // SIDE) % SIDE) * SIDE + (x + o % SIDE) % SIDE

    def column(dz):
        return (g, ((z + dz) % SIDE) * 2 + core)

    def row_copy(o):
        return pltpu.make_async_remote_copy(
            src_ref=send_ref.at[o], dst_ref=xt_ref.at[o], send_sem=row_s.at[o],
            recv_sem=row_r.at[o], device_id=(plane(o), m), device_id_type=MESH)

    def cent_copy(dz):
        return pltpu.make_async_remote_copy(
            src_ref=cent_ref, dst_ref=cbuf_ref.at[z], send_sem=cent_s.at[dz],
            recv_sem=cent_r.at[dz], device_id=column(dz), device_id_type=MESH)

    def fwd_copy(o):
        return pltpu.make_async_remote_copy(
            src_ref=xt_ref.at[o], dst_ref=xt_ref.at[CLUSTERS + o], send_sem=fwd_s.at[o],
            recv_sem=fwd_r.at[o], device_id=partner, device_id_type=MESH)

    def stat_copy(b):
        return pltpu.make_async_remote_copy(
            src_ref=stat_ref.at[b], dst_ref=peer_ref.at[(b + CLUSTERS) % BLOCKS],
            send_sem=stat_s.at[b], recv_sem=stat_r.at[(b + CLUSTERS) % BLOCKS],
            device_id=partner, device_id_type=MESH)

    def ring_copy(way, t):
        return pltpu.make_async_remote_copy(
            src_ref=rs_ref.at[way, t], dst_ref=rr_ref.at[way, t], send_sem=ring_s.at[way, t],
            recv_sem=ring_r.at[way, t], device_id=column(1 if way == 0 else SIDE - 1),
            device_id_type=MESH)

    barrier = pltpu.get_barrier_semaphore()

    @pl.loop(1, CLUSTERS)
    def _(o):
        pl.semaphore_signal(barrier, inc=1, device_id=(plane(o), m), device_id_type=MESH)

    for dz in range(1, SIDE):
        pl.semaphore_signal(barrier, inc=1, device_id=column(dz), device_id_type=MESH)
    pl.semaphore_signal(barrier, inc=1, device_id=partner, device_id_type=MESH)

    ranks(ids_ref[...], r_ref)
    for i in range(ROWS // 256):
        embt_ref[:, i * 256 : (i + 1) * 256] = emb_ref[i * 256 : (i + 1) * 256, :].T
    pl.semaphore_wait(barrier, CLUSTERS - 1 + SIDE - 1 + 1)

    for dz in range(1, SIDE):
        cent_copy(dz).start()
    cbuf_ref[z] = cent_ref[...]

    @pl.loop(1, CLUSTERS)
    def _(step):
        o = CLUSTERS - step
        send_ref[o] = permuted(plane(o), r_ref, embt_ref)
        row_copy(o).start()

    xt_ref[0] = permuted(g, r_ref, embt_ref)

    for dz in range(1, SIDE):
        cent_copy(dz).wait_recv()
    ones = jnp.ones((D, 128), BF16)
    for zz in range(SIDE):
        c = cbuf_ref[zz].astype(F32)
        square = c * c
        high = square.astype(BF16)
        low = (square - high.astype(F32)).astype(BF16)
        norm = (jnp.dot(high, ones, preferred_element_type=F32)
                + jnp.dot(low, ones, preferred_element_type=F32))
        bias_ref[zz * OWN : (zz + 1) * OWN] = norm * (-LOG2E / math.sqrt(D))

    def visit(b):
        xb = xt_ref[b]
        tops, sums = [], []
        for kc in range(CHUNKS):
            c = cbuf_ref[kc // 2, (kc % 2) * CHUNK : (kc % 2 + 1) * CHUNK, :]
            bias = bias_ref[kc * CHUNK : (kc + 1) * CHUNK]
            score = jnp.dot(c, xb, preferred_element_type=F32)
            logit = score * (2.0 * LOG2E / math.sqrt(D)) + jnp.concatenate([bias, bias], axis=1)
            top = jnp.max(logit, axis=0, keepdims=True)
            e = jnp.exp2(logit - top)
            e_ref[kc, :, pl.ds(pl.multiple_of(b * BLOCK, BLOCK), BLOCK)] = e.astype(BF16)
            tops.append(top)
            sums.append(jnp.sum(e, axis=0, keepdims=True))
        tops = jnp.concatenate(tops, axis=0)
        sums = jnp.concatenate(sums, axis=0)
        m_ref[b] = tops
        top = jnp.max(tops, axis=0, keepdims=True)
        total = jnp.sum(sums * jnp.exp2(tops - top), axis=0, keepdims=True)
        stat_ref[b] = jnp.concatenate([top] * 4 + [total] * 4, axis=0)
        stat_copy(b).start()

    @pl.loop(0, BLOCKS)
    def _(t):
        last = t == BLOCKS - 1
        odd = t % 2 == 1
        own = ((t == 0) | odd) & jnp.logical_not(last)
        o = jnp.where(last, CLUSTERS - 1, jnp.where(own, (t + 1) // 2, t // 2 - 1))
        o = jnp.where(o == 0, 0, CLUSTERS - o)

        @pl.when(own)
        def _():
            @pl.when(o > 0)
            def _():
                row_copy(o).wait_recv()

            fwd_copy(o).start()

        @pl.when(jnp.logical_not(own))
        def _():
            fwd_copy(o).wait_recv()

        visit(jnp.where(own, o, CLUSTERS + o))

    @pl.loop(0, BLOCKS)
    def _(b):
        stat_copy((b + CLUSTERS) % BLOCKS).wait_recv()
        tops = m_ref[b]
        mine, theirs = stat_ref[b], peer_ref[b]
        top = jnp.maximum(mine[0:1], theirs[0:1])
        total = (mine[4:5] * jnp.exp2(mine[0:1] - top)
                 + theirs[4:5] * jnp.exp2(theirs[0:1] - top))
        f_ref[b] = jnp.exp2(tops - top) / total

    def weighted(kc):
        @pl.loop(0, BLOCKS // 4)
        def _(q):
            parts = []
            for i in range(4):
                f = f_ref[q * 4 + i, pl.ds(kc, 1), :]
                high = f.astype(BF16).astype(F32)
                rows = xt_ref[q * 4 + i].astype(F32) * f
                rest = jnp.concatenate(
                    [high, f - high, jnp.zeros((14, BLOCK), F32)], axis=0)
                parts.append(jnp.concatenate([rows, rest], axis=0).astype(BF16))
            lhs = jnp.concatenate(parts, axis=1)
            rhs = e_ref[kc, :, pl.ds(pl.multiple_of(q * 4 * BLOCK, 4 * BLOCK), 4 * BLOCK)]
            part = lax.dot_general(lhs, rhs, NT, preferred_element_type=F32)

            @pl.when(q == 0)
            def _():
                acc_ref[...] = part

            @pl.when(q > 0)
            def _():
                acc_ref[...] += part

        return (acc_ref[0:D],
                jnp.broadcast_to(acc_ref[D : D + 1] + acc_ref[D + 1 : D + 2], (8, CHUNK)))

    @pl.loop(0, SIDE)
    def _(t):
        for way in range(2):
            owner = (z + SIDE - 1 - t) % SIDE if way == 0 else (z + 1 + t) % SIDE
            w, mass = weighted(owner * 2 + way)
            acc_ref[0:D] = w
            acc_ref[D : D + 8] = mass

            @pl.when(t > 0)
            def _():
                ring_copy(way, t - 1).wait_recv()
                acc_ref[0:WROWS] += rr_ref[way, t - 1]

            @pl.when(t < SIDE - 1)
            def _():
                rs_ref[way, t] = acc_ref[0:WROWS]
                ring_copy(way, t).start()

            @pl.when(t == SIDE - 1)
            def _():
                rows = slice(way * CHUNK, (way + 1) * CHUNK)
                mass = acc_ref[D : D + 1]
                mass_ref[:, rows] = mass
                den = jnp.broadcast_to(mass + PRIOR_MASS, (128, CHUNK)).T
                den = jnp.concatenate([den, den], axis=1)
                prior = PRIOR_MASS * cent_ref[rows, :].astype(F32)
                out_ref[rows, :] = (acc_ref[0:D].T + prior) / den

    for way in range(2):
        for t in range(SIDE - 1):
            ring_copy(way, t).wait_send()
    for dz in range(1, SIDE):
        cent_copy(dz).wait_send()

    @pl.loop(0, CLUSTERS)
    def _(o):
        @pl.when(o > 0)
        def _():
            row_copy(o).wait_send()

        fwd_copy(o).wait_send()

    @pl.loop(0, BLOCKS)
    def _(b):
        stat_copy(b).wait_send()


def local(embeddings, cluster_ids, centroids):
    dma = pltpu.SemaphoreType.DMA
    own = centroids[0]
    out, mass = pl.pallas_call(
        kernel,
        out_shape=(jax.ShapeDtypeStruct((OWN, D), F32), jax.ShapeDtypeStruct((1, OWN), F32)),
        in_specs=[pl.BlockSpec(memory_space=pltpu.VMEM)] * 3,
        out_specs=(pl.BlockSpec(memory_space=pltpu.VMEM),) * 2,
        scratch_shapes=[
            pltpu.VMEM((D, ROWS), BF16),
            pltpu.VMEM((CLUSTERS, D, BLOCK), BF16),
            pltpu.VMEM((BLOCKS, D, BLOCK), BF16),
            pltpu.VMEM((CLUSTERS, 32, 128), F32),
            pltpu.VMEM((SIDE, OWN, D), BF16),
            pltpu.VMEM((SIDE * OWN, 128), F32),
            pltpu.VMEM((CHUNKS, CHUNK, BLOCKS * BLOCK), BF16),
            pltpu.VMEM((BLOCKS, CHUNKS, BLOCK), F32),
            pltpu.VMEM((8, 128), F32),
            pltpu.VMEM((BLOCKS, 8, BLOCK), F32),
            pltpu.VMEM((BLOCKS, 8, BLOCK), F32),
            pltpu.VMEM((BLOCKS, CHUNKS, BLOCK), F32),
            pltpu.VMEM((D + 16, CHUNK), F32),
            pltpu.VMEM((2, SIDE - 1, WROWS, CHUNK), F32),
            pltpu.VMEM((2, SIDE - 1, WROWS, CHUNK), F32),
            dma((CLUSTERS,)), dma((CLUSTERS,)), dma((SIDE,)), dma((SIDE,)),
            dma((CLUSTERS,)), dma((CLUSTERS,)), dma((BLOCKS,)), dma((BLOCKS,)),
            dma((2, SIDE - 1)), dma((2, SIDE - 1)),
        ],
        compiler_params=pltpu.CompilerParams(
            collective_id=0, has_side_effects=True, vmem_limit_bytes=60 << 20),
        cost_estimate=pl.CostEstimate(flops=24 << 30, bytes_accessed=4 << 20, transcendentals=1 << 24),
        name="soft_kmeans",
    )(embeddings, cluster_ids.reshape(32, 128), own)
    return out[None], mass


def solution(mesh):
    placed = (P(("group", "member"), None), P(("group", "member")), P("group", "member", None))
    return jax.shard_map(
        local,
        mesh=mesh,
        in_specs=placed,
        out_specs=(P("group", "member", None), P("group", "member")),
        check_vma=False,
    )
```

```python
import functools
import math

import jax
import jax.numpy as jnp
from jax import lax
from jax.experimental import pallas as pl
from jax.experimental.pallas import tpu as pltpu
from jax.sharding import PartitionSpec as P

F32, BF16 = jnp.float32, jnp.bfloat16
MESH = pl.DeviceIdType.MESH
NT = (((1,), (1,)), ((), ()))
LOG2E = 1.4426950408889634
PRIOR_MASS = 1.0

SIDE = 4
CLUSTERS = 16
D = 256
ROWS = 4096
BLOCK = 256
BLOCKS = 32
CHUNK = 256
CHUNKS = 8
OWN = 512
LEVELS = 32767.0


def iota(shape, dim):
    return lax.broadcasted_iota(jnp.int32, shape, dim)


def ranks(ids, r_ref):
    upper = (iota((128, 128), 0) <= iota((128, 128), 1)).astype(F32).astype(BF16)
    ones = jnp.ones((128, 128), BF16)
    ri, ci = iota((128, 128), 0), iota((128, 128), 1)
    before = ((ri // 32 == ci // 32) & (ci < ri)).astype(F32).astype(BF16)
    for quad in range(CLUSTERS // 4):
        eq = jnp.concatenate(
            [(ids == quad * 4 + i).astype(F32) for i in range(4)], axis=0
        )
        hot = eq.astype(BF16)
        inside = jnp.dot(hot, upper, preferred_element_type=F32)
        totals = jnp.dot(hot, ones, preferred_element_type=F32).astype(BF16)
        ahead = jnp.dot(before, totals, preferred_element_type=F32)
        rank = jnp.where(eq > 0.5, inside + ahead - 1.0, -1.0)
        for i in range(4):
            r_ref[quad * 4 + i] = rank[i * 32 : (i + 1) * 32]


def permuted(clusters, r_ref, embt_ref):
    place = iota((BLOCK, 128), 0).astype(F32).astype(BF16)
    one, zero = jnp.ones_like(place), jnp.zeros_like(place)
    both = []
    for cluster in clusters:
        rank = r_ref[cluster]
        hots = []
        for t in range(ROWS // 128):
            row = jnp.broadcast_to(rank[t : t + 1], (BLOCK, 128)).astype(BF16)
            hots.append(jnp.where(row == place, one, zero))
        both.append(jnp.concatenate(hots, axis=1))
    hot = jnp.concatenate(both, axis=0)
    out = lax.dot_general(embt_ref[...], hot, NT, preferred_element_type=F32)
    return out.astype(BF16)


def places():
    pairs = [(0, 1)]
    pairs += [(t + 1, CLUSTERS + t - 1) for t in range(1, CLUSTERS - 1)]
    return pairs + [(BLOCKS - 2, BLOCKS - 1)]


def kernel(emb_hbm, ids_ref, cent_ref, out_ref, mass_ref,
           emb_ref, embt_ref, send_ref, xt_ref, r_ref, cbuf_ref, bias_ref, e_ref,
           m_ref, s_ref, stat_ref, peer_ref, f_ref, acc_ref, qs_ref, qr_ref, ss_ref, sr_ref,
           row_s, row_r, cent_s, cent_r, fwd_s, fwd_r, stat_s, stat_r,
           sum_s, sum_r, side_s, side_r, emb_s):
    g, m = lax.axis_index("group"), lax.axis_index("member")
    y, x = g // SIDE, g % SIDE
    z, core = m // 2, m % 2
    partner = (g, z * 2 + 1 - core)

    def plane(j):
        o = (CLUSTERS - j) % CLUSTERS
        return ((y + o // SIDE) % SIDE) * SIDE + (x + o % SIDE) % SIDE

    def column(dz):
        return (g, ((z + dz) % SIDE) * 2 + core)

    def row_copy(j):
        return pltpu.make_async_remote_copy(
            src_ref=send_ref.at[j], dst_ref=xt_ref.at[j], send_sem=row_s.at[j],
            recv_sem=row_r.at[j], device_id=(plane(j), m), device_id_type=MESH)

    def cent_copy(dz):
        return pltpu.make_async_remote_copy(
            src_ref=cent_ref, dst_ref=cbuf_ref.at[z], send_sem=cent_s.at[dz],
            recv_sem=cent_r.at[dz], device_id=column(dz), device_id_type=MESH)

    def fwd_copy(j):
        return pltpu.make_async_remote_copy(
            src_ref=xt_ref.at[j], dst_ref=xt_ref.at[CLUSTERS + j], send_sem=fwd_s.at[j],
            recv_sem=fwd_r.at[j], device_id=partner, device_id_type=MESH)

    def stat_copy(half):
        return pltpu.make_async_remote_copy(
            src_ref=stat_ref.at[pl.ds(half * CLUSTERS, CLUSTERS)],
            dst_ref=peer_ref.at[pl.ds((1 - half) * CLUSTERS, CLUSTERS)],
            send_sem=stat_s.at[half], recv_sem=stat_r.at[half],
            device_id=partner, device_id_type=MESH)

    def sum_copy(dz, part):
        return pltpu.make_async_remote_copy(
            src_ref=qs_ref.at[dz - 1, part], dst_ref=qr_ref.at[dz - 1, part],
            send_sem=sum_s.at[dz - 1, part], recv_sem=sum_r.at[dz - 1, part],
            device_id=column(dz), device_id_type=MESH)

    def side_copy(dz, part):
        return pltpu.make_async_remote_copy(
            src_ref=ss_ref.at[dz - 1, part], dst_ref=sr_ref.at[dz - 1, part],
            send_sem=side_s.at[dz - 1, part], recv_sem=side_r.at[dz - 1, part],
            device_id=column(dz), device_id_type=MESH)

    load = pltpu.make_async_copy(emb_hbm, emb_ref, emb_s)
    load.start()
    barrier = pltpu.get_barrier_semaphore()

    @pl.loop(1, CLUSTERS)
    def _(j):
        pl.semaphore_signal(barrier, inc=1, device_id=(plane(j), m), device_id_type=MESH)

    for dz in range(1, SIDE):
        pl.semaphore_signal(barrier, inc=1, device_id=column(dz), device_id_type=MESH)
    pl.semaphore_signal(barrier, inc=1, device_id=partner, device_id_type=MESH)

    ranks(ids_ref[...], r_ref)
    load.wait()

    @pl.loop(0, ROWS // 512)
    def _(i):
        part = pl.ds(pl.multiple_of(i * 512, 512), 512)
        embt_ref[:, part] = emb_ref[part, :].T

    pl.semaphore_wait(barrier, CLUSTERS - 1 + SIDE - 1 + 1)

    for dz in range(1, SIDE):
        cent_copy(dz).start()
    cbuf_ref[z] = cent_ref[...]

    @pl.loop(0, CLUSTERS // 2)
    def _(i):
        j = 2 * i + 1
        pair = permuted((plane(j), plane((j + 1) % CLUSTERS)), r_ref, embt_ref)
        send_ref[j] = pair[:, :BLOCK]
        row_copy(j).start()

        @pl.when(j < CLUSTERS - 1)
        def _():
            send_ref[j + 1] = pair[:, BLOCK:]
            row_copy(j + 1).start()

        @pl.when(j == CLUSTERS - 1)
        def _():
            xt_ref[0] = pair[:, BLOCK:]

    fwd_copy(0).start()

    for dz in range(1, SIDE):
        cent_copy(dz).wait_recv()
    ones = jnp.ones((D, 128), BF16)

    @pl.loop(0, SIDE)
    def _(zz):
        c = cbuf_ref[zz].astype(F32)
        square = c * c
        high = square.astype(BF16)
        low = (square - high.astype(F32)).astype(BF16)
        norm = (jnp.dot(high, ones, preferred_element_type=F32)
                + jnp.dot(low, ones, preferred_element_type=F32))
        bias_ref[pl.ds(pl.multiple_of(zz * OWN, OWN), OWN)] = norm * (-LOG2E / math.sqrt(D))

    def combine(half):
        slots = slice(half * CLUSTERS, (half + 1) * CLUSTERS)
        tops, sums = m_ref[slots], s_ref[slots]
        top = jnp.max(tops, axis=1, keepdims=True)
        total = jnp.sum(sums * jnp.exp2(tops - top), axis=1, keepdims=True)
        stat_ref[slots] = jnp.concatenate([top] * 4 + [total] * 4, axis=1)
        stat_copy(half).start()

    @pl.loop(0, CLUSTERS)
    def _(t):
        first, last = t == 0, t == CLUSTERS - 1
        a = jnp.where(first, 0, jnp.where(last, BLOCKS - 2, t + 1))
        b = jnp.where(first, 1, jnp.where(last, BLOCKS - 1, CLUSTERS + t - 1))

        @pl.when(jnp.logical_not(last))
        def _():
            row_copy(t + 1).wait_recv()
            fwd_copy(t + 1).start()

        @pl.when(t > 0)
        def _():
            fwd_copy(t - 1).wait_recv()

        @pl.when(last)
        def _():
            fwd_copy(CLUSTERS - 1).wait_recv()
            combine(0)

        xb = jnp.concatenate([xt_ref[a], xt_ref[b]], axis=1)
        columns = pl.ds(pl.multiple_of(t * 2 * BLOCK, 2 * BLOCK), 2 * BLOCK)
        tops, sums = [], []
        for kc in range(CHUNKS):
            c = cbuf_ref[kc // 2, (kc % 2) * CHUNK : (kc % 2 + 1) * CHUNK, :]
            bias = bias_ref[kc * CHUNK : (kc + 1) * CHUNK]
            score = jnp.dot(c, xb, preferred_element_type=F32)
            logit = score * (2.0 * LOG2E / math.sqrt(D)) + jnp.concatenate([bias] * 4, axis=1)
            top = jnp.max(logit, axis=0, keepdims=True)
            e = jnp.exp2(logit - top)
            e_ref[kc, :, columns] = e.astype(BF16)
            tops.append(top)
            sums.append(jnp.sum(e, axis=0, keepdims=True))
        tops = jnp.concatenate(tops, axis=0)
        sums = jnp.concatenate(sums, axis=0)
        m_ref[a], m_ref[b] = tops[:, :BLOCK], tops[:, BLOCK:]
        s_ref[a], s_ref[b] = sums[:, :BLOCK], sums[:, BLOCK:]

    combine(1)
    for half in range(2):
        stat_copy(half).wait_recv()
        slots = slice((1 - half) * CLUSTERS, (2 - half) * CLUSTERS)
        mine, theirs = stat_ref[slots], peer_ref[slots]
        top = jnp.maximum(mine[:, 0:1], theirs[:, 0:1])
        total = (mine[:, 4:5] * jnp.exp2(mine[:, 0:1] - top)
                 + theirs[:, 4:5] * jnp.exp2(theirs[:, 0:1] - top))
        f_ref[slots] = jnp.exp2(m_ref[slots] - top) * (1.0 / total)

    order = [slot for pair in places() for slot in pair]

    def weighted(kc):
        parts = []
        for slot in order:
            f = f_ref[slot, pl.ds(kc, 1), :]
            high = f.astype(BF16).astype(F32)
            rows = xt_ref[slot].astype(F32) * f
            rest = jnp.concatenate([high, f - high, jnp.zeros((14, BLOCK), F32)], axis=0)
            parts.append(jnp.concatenate([rows, rest], axis=0).astype(BF16))
        lhs = jnp.concatenate(parts, axis=1)
        acc_ref[...] = lax.dot_general(lhs, e_ref[kc], NT, preferred_element_type=F32)

    @pl.loop(0, 2 * SIDE)
    def _(u):
        turn, part = u // 2, u % 2
        dz = jnp.where(turn == 0, 2, jnp.where(turn == 1, 1, jnp.where(turn == 2, 3, 0)))
        weighted(((z + dz) % SIDE) * 2 + part)
        mass = acc_ref[D : D + 1] + acc_ref[D + 1 : D + 2]

        @pl.when(turn < SIDE - 1)
        def _():
            w = acc_ref[0:D]
            peak = jnp.maximum(jnp.max(jnp.abs(w), axis=0, keepdims=True), 1e-30)
            q = jnp.round(w * (LEVELS / peak)).astype(jnp.int32)
            qs_ref[dz - 1, part] = q.astype(jnp.int16)
            sum_copy(dz, part).start()
            ss_ref[dz - 1, part] = jnp.concatenate([peak * (1.0 / LEVELS)] * 4 + [mass] * 4, axis=0)
            side_copy(dz, part).start()

        @pl.when(turn == SIDE - 1)
        def _():
            total, w = mass, acc_ref[0:D]
            for away in range(1, SIDE):
                side_copy(away, part).wait_recv()
                sum_copy(away, part).wait_recv()
                side = sr_ref[away - 1, part]
                total = total + side[4:5]
                w = w + qr_ref[away - 1, part].astype(jnp.int32).astype(F32) * side[0:1]
            rows = pl.ds(pl.multiple_of(part * CHUNK, CHUNK), CHUNK)
            mass_ref[:, rows] = total
            den = jnp.broadcast_to(total + PRIOR_MASS, (128, CHUNK)).T
            den = jnp.concatenate([den, den], axis=1)
            prior = PRIOR_MASS * cent_ref[rows, :].astype(F32)
            out_ref[rows, :] = (w.T + prior) / den

    for part in range(2):
        for dz in range(1, SIDE):
            side_copy(dz, part).wait_send()
            sum_copy(dz, part).wait_send()
    for dz in range(1, SIDE):
        cent_copy(dz).wait_send()
    for half in range(2):
        stat_copy(half).wait_send()
    fwd_copy(0).wait_send()

    @pl.loop(1, CLUSTERS)
    def _(j):
        row_copy(j).wait_send()
        fwd_copy(j).wait_send()


def deliver(out_in, mass_in, out_ref, mass_ref):
    out_ref[...] = out_in[...]
    mass_ref[...] = mass_in[...]


def local(embeddings, cluster_ids, centroids):
    dma = pltpu.SemaphoreType.DMA
    own = centroids[0]
    out, mass = pl.pallas_call(
        kernel,
        out_shape=(jax.ShapeDtypeStruct((OWN, D), F32), jax.ShapeDtypeStruct((1, OWN), F32)),
        in_specs=[pl.BlockSpec(memory_space=pl.ANY)] + [pl.BlockSpec(memory_space=pltpu.VMEM)] * 2,
        out_specs=(pl.BlockSpec(memory_space=pltpu.VMEM),) * 2,
        scratch_shapes=[
            pltpu.VMEM((ROWS, D), BF16),
            pltpu.VMEM((D, ROWS), BF16),
            pltpu.VMEM((CLUSTERS, D, BLOCK), BF16),
            pltpu.VMEM((BLOCKS, D, BLOCK), BF16),
            pltpu.VMEM((CLUSTERS, 32, 128), F32),
            pltpu.VMEM((SIDE, OWN, D), BF16),
            pltpu.VMEM((SIDE * OWN, 128), F32),
            pltpu.VMEM((CHUNKS, CHUNK, BLOCKS * BLOCK), BF16),
            pltpu.VMEM((BLOCKS, CHUNKS, BLOCK), F32),
            pltpu.VMEM((BLOCKS, CHUNKS, BLOCK), F32),
            pltpu.VMEM((BLOCKS, 8, BLOCK), F32),
            pltpu.VMEM((BLOCKS, 8, BLOCK), F32),
            pltpu.VMEM((BLOCKS, CHUNKS, BLOCK), F32),
            pltpu.VMEM((D + 16, CHUNK), F32),
            pltpu.VMEM((SIDE - 1, 2, D, CHUNK), jnp.int16),
            pltpu.VMEM((SIDE - 1, 2, D, CHUNK), jnp.int16),
            pltpu.VMEM((SIDE - 1, 2, 8, CHUNK), F32),
            pltpu.VMEM((SIDE - 1, 2, 8, CHUNK), F32),
            dma((CLUSTERS,)), dma((CLUSTERS,)), dma((SIDE,)), dma((SIDE,)),
            dma((CLUSTERS,)), dma((CLUSTERS,)), dma((2,)), dma((2,)),
            dma((SIDE - 1, 2)), dma((SIDE - 1, 2)), dma((SIDE - 1, 2)), dma((SIDE - 1, 2)), dma,
        ],
        compiler_params=pltpu.CompilerParams(
            collective_id=0, has_side_effects=True, vmem_limit_bytes=60 << 20),
        cost_estimate=pl.CostEstimate(flops=24 << 30, bytes_accessed=4 << 20, transcendentals=1 << 24),
        name="soft_kmeans",
    )(embeddings, cluster_ids.reshape(32, 128), own)
    shapes = (jax.ShapeDtypeStruct((OWN, D), F32), jax.ShapeDtypeStruct((1, OWN), F32))
    out, mass = pl.pallas_call(
        deliver,
        out_shape=shapes,
        in_specs=[pl.BlockSpec(memory_space=pltpu.VMEM)] * 2,
        out_specs=(pl.BlockSpec(memory_space=pltpu.VMEM),) * 2,
        name="deliver",
    )(out, mass)
    return out[None], mass


def solution(mesh):
    placed = (P(("group", "member"), None), P(("group", "member")), P("group", "member", None))
    return jax.shard_map(
        local,
        mesh=mesh,
        in_specs=placed,
        out_specs=(P("group", "member", None), P("group", "member")),
        check_vma=False,
    )
```

```python
import functools
import math

import jax
import jax.numpy as jnp
from jax import lax
from jax.experimental import pallas as pl
from jax.experimental.pallas import tpu as pltpu
from jax.sharding import PartitionSpec as P

F32, BF16 = jnp.float32, jnp.bfloat16
MESH = pl.DeviceIdType.MESH
NT = (((1,), (1,)), ((), ()))
LOG2E = 1.4426950408889634
PRIOR_MASS = 1.0

SIDE = 4
CLUSTERS = 16
D = 256
ROWS = 4096
BLOCK = 256
BLOCKS = 32
STEP_OF = (0, 1, 3, 4, 12, 2, 8, 5, 15, 7, 13, 6, 14, 9, 11, 10)
VISITS = 8
CHUNK = 256
CHUNKS = 8
OWN = 512
STEPS = 8
LEVELS = 32767.0


def iota(shape, dim):
    return lax.broadcasted_iota(jnp.int32, shape, dim)


def ranks(ids, r_ref):
    upper = (iota((128, 128), 0) <= iota((128, 128), 1)).astype(F32).astype(BF16)
    ones = jnp.ones((128, 128), BF16)
    ri, ci = iota((128, 128), 0), iota((128, 128), 1)
    before = ((ri // 32 == ci // 32) & (ci < ri)).astype(F32).astype(BF16)
    for quad in range(CLUSTERS // 4):
        eq = jnp.concatenate(
            [(ids == quad * 4 + i).astype(F32) for i in range(4)], axis=0
        )
        hot = eq.astype(BF16)
        inside = jnp.dot(hot, upper, preferred_element_type=F32)
        totals = jnp.dot(hot, ones, preferred_element_type=F32).astype(BF16)
        ahead = jnp.dot(before, totals, preferred_element_type=F32)
        rank = jnp.where(eq > 0.5, inside + ahead - 1.0, -1.0)
        for i in range(4):
            r_ref[quad * 4 + i] = rank[i * 32 : (i + 1) * 32]


def permuted(clusters, r_ref, embt_ref):
    place = iota((BLOCK, 128), 0).astype(F32).astype(BF16)
    one, zero = jnp.ones_like(place), jnp.zeros_like(place)
    both = []
    for cluster in clusters:
        rank = r_ref[cluster]
        hots = []
        for t in range(ROWS // 128):
            row = jnp.broadcast_to(rank[t : t + 1], (BLOCK, 128)).astype(BF16)
            hots.append(jnp.where(row == place, one, zero))
        both.append(jnp.concatenate(hots, axis=1))
    hot = jnp.concatenate(both, axis=0)
    out = lax.dot_general(embt_ref[...], hot, NT, preferred_element_type=F32)
    return out.astype(BF16)


def visits():
    rounds = [(0, 1, 2, 3)]
    rounds += [(2 * i + 2, 2 * i + 3, 2 * i + 14, 2 * i + 15) for i in range(1, 7)]
    return rounds + [(28, 29, 30, 31)]


def kernel(emb_hbm, ids_ref, cent_ref, out_ref, mass_ref,
           emb_ref, embt_ref, send_ref, xt_ref, r_ref, cbuf_ref, bias_ref, e_ref,
           m_ref, s_ref, stat_ref, peer_ref, f_ref, acc_ref, qs_ref, qr_ref, ss_ref, sr_ref,
           row_s, row_r, cent_s, cent_r, fwd_s, fwd_r, stat_s, stat_r,
           sum_s, sum_r, side_s, side_r, emb_s):
    g, m = lax.axis_index("group"), lax.axis_index("member")
    y, x = g // SIDE, g % SIDE
    z, core = m // 2, m % 2
    partner = (g, z * 2 + 1 - core)

    def plane(j):
        o = sum(jnp.where(j == k, STEP_OF[k], 0) for k in range(CLUSTERS))
        return ((y + o // SIDE) % SIDE) * SIDE + (x + o % SIDE) % SIDE

    def column(dz):
        return (g, ((z + dz) % SIDE) * 2 + core)

    def row_copy(j):
        return pltpu.make_async_remote_copy(
            src_ref=send_ref.at[j], dst_ref=xt_ref.at[j], send_sem=row_s.at[j],
            recv_sem=row_r.at[j], device_id=(plane(j), m), device_id_type=MESH)

    def cent_copy(dz):
        return pltpu.make_async_remote_copy(
            src_ref=cent_ref, dst_ref=cbuf_ref.at[z], send_sem=cent_s.at[dz],
            recv_sem=cent_r.at[dz], device_id=column(dz), device_id_type=MESH)

    def fwd_copy(j):
        return pltpu.make_async_remote_copy(
            src_ref=xt_ref.at[j], dst_ref=xt_ref.at[CLUSTERS + j], send_sem=fwd_s.at[j],
            recv_sem=fwd_r.at[j], device_id=partner, device_id_type=MESH)

    def stat_copy(half):
        return pltpu.make_async_remote_copy(
            src_ref=stat_ref.at[pl.ds(half * CLUSTERS, CLUSTERS)],
            dst_ref=peer_ref.at[pl.ds((1 - half) * CLUSTERS, CLUSTERS)],
            send_sem=stat_s.at[half], recv_sem=stat_r.at[half],
            device_id=partner, device_id_type=MESH)

    def sum_copy(u):
        return pltpu.make_async_remote_copy(
            src_ref=qs_ref.at[u], dst_ref=qr_ref.at[u], send_sem=sum_s.at[u],
            recv_sem=sum_r.at[u], device_id=column(1 + 2 * (u % 2)), device_id_type=MESH)

    def side_copy(u):
        return pltpu.make_async_remote_copy(
            src_ref=ss_ref.at[u], dst_ref=sr_ref.at[u], send_sem=side_s.at[u],
            recv_sem=side_r.at[u], device_id=column(1 + 2 * (u % 2)), device_id_type=MESH)

    load = pltpu.make_async_copy(emb_hbm, emb_ref, emb_s)
    load.start()
    barrier = pltpu.get_barrier_semaphore()

    @pl.loop(1, CLUSTERS)
    def _(j):
        pl.semaphore_signal(barrier, inc=1, device_id=(plane(j), m), device_id_type=MESH)

    for dz in range(1, SIDE):
        pl.semaphore_signal(barrier, inc=1, device_id=column(dz), device_id_type=MESH)
    pl.semaphore_signal(barrier, inc=1, device_id=partner, device_id_type=MESH)

    ranks(ids_ref[...], r_ref)
    load.wait()

    @pl.loop(0, ROWS // 512)
    def _(i):
        part = pl.ds(pl.multiple_of(i * 512, 512), 512)
        embt_ref[:, part] = emb_ref[part, :].T

    pl.semaphore_wait(barrier, CLUSTERS - 1 + SIDE - 1 + 1)

    for dz in range(1, SIDE):
        cent_copy(dz).start()
    cbuf_ref[z] = cent_ref[...]

    @pl.loop(0, CLUSTERS // 2)
    def _(i):
        j = 2 * i + 1
        pair = permuted((plane(j), plane((j + 1) % CLUSTERS)), r_ref, embt_ref)
        send_ref[j] = pair[:, :BLOCK]
        row_copy(j).start()

        @pl.when(j < CLUSTERS - 1)
        def _():
            send_ref[j + 1] = pair[:, BLOCK:]
            row_copy(j + 1).start()

        @pl.when(j == CLUSTERS - 1)
        def _():
            xt_ref[0] = pair[:, BLOCK:]

    fwd_copy(0).start()

    for dz in range(1, SIDE):
        cent_copy(dz).wait_recv()
    ones = jnp.ones((D, 128), BF16)

    @pl.loop(0, SIDE)
    def _(zz):
        c = cbuf_ref[zz].astype(F32)
        square = c * c
        high = square.astype(BF16)
        low = (square - high.astype(F32)).astype(BF16)
        norm = (jnp.dot(high, ones, preferred_element_type=F32)
                + jnp.dot(low, ones, preferred_element_type=F32))
        bias_ref[pl.ds(pl.multiple_of(zz * OWN, OWN), OWN)] = norm * (-LOG2E / math.sqrt(D))

    def combine(half):
        slots = slice(half * CLUSTERS, (half + 1) * CLUSTERS)
        tops, sums = m_ref[slots], s_ref[slots]
        top = jnp.max(tops, axis=1, keepdims=True)
        total = jnp.sum(sums * jnp.exp2(tops - top), axis=1, keepdims=True)
        stat_ref[slots] = jnp.concatenate([top] * 4 + [total] * 4, axis=1)
        stat_copy(half).start()

    @pl.loop(0, VISITS)
    def _(i):
        first, last = i == 0, i == VISITS - 1
        one = jnp.where(first, 0, jnp.where(last, 28, 2 * i + 2))
        two = jnp.where(first, 2, jnp.where(last, 30, 2 * i + 14))
        slots = (one, one + 1, two, two + 1)

        @pl.when(first)
        def _():
            row_copy(1).wait_recv()
            fwd_copy(1).start()

        @pl.when(jnp.logical_not(last))
        def _():
            for k in range(2):
                row_copy(2 * i + 2 + k).wait_recv()
                fwd_copy(2 * i + 2 + k).start()

        @pl.when(i > 0)
        def _():
            for k in range(2):
                fwd_copy(2 * i - 2 + k).wait_recv()

        @pl.when(last)
        def _():
            for k in range(2):
                fwd_copy(CLUSTERS - 2 + k).wait_recv()
            combine(0)

        xb = jnp.concatenate([xt_ref[slot] for slot in slots], axis=1)
        columns = pl.ds(pl.multiple_of(i * 4 * BLOCK, 4 * BLOCK), 4 * BLOCK)
        tops, sums = [], []
        for kc in range(CHUNKS):
            c = cbuf_ref[kc // 2, (kc % 2) * CHUNK : (kc % 2 + 1) * CHUNK, :]
            bias = bias_ref[kc * CHUNK : (kc + 1) * CHUNK]
            score = jnp.dot(c, xb, preferred_element_type=F32)
            logit = score * (2.0 * LOG2E / math.sqrt(D)) + jnp.concatenate([bias] * 8, axis=1)
            top = jnp.max(logit, axis=0, keepdims=True)
            e = jnp.exp2(logit - top)
            e_ref[kc, :, columns] = e.astype(BF16)
            tops.append(top)
            sums.append(jnp.sum(e, axis=0, keepdims=True))
        tops = jnp.concatenate(tops, axis=0)
        sums = jnp.concatenate(sums, axis=0)
        for k, slot in enumerate(slots):
            m_ref[slot] = tops[:, k * BLOCK : (k + 1) * BLOCK]
            s_ref[slot] = sums[:, k * BLOCK : (k + 1) * BLOCK]

    combine(1)
    for half in range(2):
        stat_copy(half).wait_recv()
        slots = slice((1 - half) * CLUSTERS, (2 - half) * CLUSTERS)
        mine, theirs = stat_ref[slots], peer_ref[slots]
        top = jnp.maximum(mine[:, 0:1], theirs[:, 0:1])
        total = (mine[:, 4:5] * jnp.exp2(mine[:, 0:1] - top)
                 + theirs[:, 4:5] * jnp.exp2(theirs[:, 0:1] - top))
        f_ref[slots] = jnp.exp2(m_ref[slots] - top) * (1.0 / total)

    order = [slot for four in visits() for slot in four]

    def weighted(kc, acc):
        parts = []
        for slot in order:
            f = f_ref[slot, pl.ds(kc, 1), :]
            high = f.astype(BF16).astype(F32)
            rows = xt_ref[slot].astype(F32) * f
            rest = jnp.concatenate([high, f - high, jnp.zeros((14, BLOCK), F32)], axis=0)
            parts.append(jnp.concatenate([rows, rest], axis=0).astype(BF16))
        lhs = jnp.concatenate(parts, axis=1)
        acc[...] = lax.dot_general(lhs, e_ref[kc], NT, preferred_element_type=F32)

    def absorb(acc, slot):
        side_copy(slot).wait_recv()
        sum_copy(slot).wait_recv()
        side = sr_ref[slot]
        acc[0:D] += qr_ref[slot].astype(jnp.int32).astype(F32) * side[0:1]
        acc[D : D + 8] += jnp.broadcast_to(side[4:5], (8, CHUNK))

    @pl.loop(0, STEPS)
    def _(u):
        pair, odd = u // 2, u % 2
        hops = jnp.where(pair == 0, 2, jnp.where(pair == 3, 0, 1 + 2 * odd))
        part = jnp.where(pair == 1, 1 - odd, odd)
        acc = acc_ref.at[odd]
        weighted(((z + hops) % SIDE) * 2 + part, acc)
        mass = acc[D : D + 1] + acc[D + 1 : D + 2]
        acc[D : D + 8] = jnp.broadcast_to(mass, (8, CHUNK))

        @pl.when(pair == 2)
        def _():
            absorb(acc, u - 4)

        @pl.when(pair < 3)
        def _():
            w = acc[0:D]
            peak = jnp.maximum(jnp.max(jnp.abs(w), axis=0, keepdims=True), 1e-30)
            q = jnp.round(w * (LEVELS / peak)).astype(jnp.int32)
            qs_ref[u] = q.astype(jnp.int16)
            sum_copy(u).start()
            ss_ref[u, 0:4] = jnp.broadcast_to(peak * (1.0 / LEVELS), (4, CHUNK))
            ss_ref[u, 4:8] = acc[D : D + 4]
            side_copy(u).start()

    @pl.loop(0, 2)
    def _(part):
        acc = acc_ref.at[part]
        absorb(acc, 3 - part)
        absorb(acc, 4 + part)
        rows = pl.ds(pl.multiple_of(part * CHUNK, CHUNK), CHUNK)
        total = acc[D : D + 1]
        mass_ref[:, rows] = total
        den = jnp.broadcast_to(total + PRIOR_MASS, (128, CHUNK)).T
        den = jnp.concatenate([den, den], axis=1)
        prior = PRIOR_MASS * cent_ref[rows, :].astype(F32)
        out_ref[rows, :] = (acc[0:D].T + prior) / den

    @pl.loop(0, STEPS - 2)
    def _(u):
        side_copy(u).wait_send()
        sum_copy(u).wait_send()

    for dz in range(1, SIDE):
        cent_copy(dz).wait_send()
    for half in range(2):
        stat_copy(half).wait_send()
    fwd_copy(0).wait_send()

    @pl.loop(1, CLUSTERS)
    def _(j):
        row_copy(j).wait_send()
        fwd_copy(j).wait_send()


def deliver(out_in, mass_in, out_ref, mass_ref):
    out_ref[...] = out_in[...]
    mass_ref[...] = mass_in[...]


def local(embeddings, cluster_ids, centroids):
    dma = pltpu.SemaphoreType.DMA
    own = centroids[0]
    out, mass = pl.pallas_call(
        kernel,
        out_shape=(jax.ShapeDtypeStruct((OWN, D), F32), jax.ShapeDtypeStruct((1, OWN), F32)),
        in_specs=[pl.BlockSpec(memory_space=pl.ANY)] + [pl.BlockSpec(memory_space=pltpu.VMEM)] * 2,
        out_specs=(pl.BlockSpec(memory_space=pltpu.VMEM),) * 2,
        scratch_shapes=[
            pltpu.VMEM((ROWS, D), BF16),
            pltpu.VMEM((D, ROWS), BF16),
            pltpu.VMEM((CLUSTERS, D, BLOCK), BF16),
            pltpu.VMEM((BLOCKS, D, BLOCK), BF16),
            pltpu.VMEM((CLUSTERS, 32, 128), F32),
            pltpu.VMEM((SIDE, OWN, D), BF16),
            pltpu.VMEM((SIDE * OWN, 128), F32),
            pltpu.VMEM((CHUNKS, CHUNK, BLOCKS * BLOCK), BF16),
            pltpu.VMEM((BLOCKS, CHUNKS, BLOCK), F32),
            pltpu.VMEM((BLOCKS, CHUNKS, BLOCK), F32),
            pltpu.VMEM((BLOCKS, 8, BLOCK), F32),
            pltpu.VMEM((BLOCKS, 8, BLOCK), F32),
            pltpu.VMEM((BLOCKS, CHUNKS, BLOCK), F32),
            pltpu.VMEM((2, D + 16, CHUNK), F32),
            pltpu.VMEM((STEPS - 2, D, CHUNK), jnp.int16),
            pltpu.VMEM((STEPS - 2, D, CHUNK), jnp.int16),
            pltpu.VMEM((STEPS - 2, 8, CHUNK), F32),
            pltpu.VMEM((STEPS - 2, 8, CHUNK), F32),
            dma((CLUSTERS,)), dma((CLUSTERS,)), dma((SIDE,)), dma((SIDE,)),
            dma((CLUSTERS,)), dma((CLUSTERS,)), dma((2,)), dma((2,)),
            dma((STEPS - 2,)), dma((STEPS - 2,)), dma((STEPS - 2,)), dma((STEPS - 2,)), dma,
        ],
        compiler_params=pltpu.CompilerParams(
            collective_id=0, has_side_effects=True, vmem_limit_bytes=60 << 20),
        cost_estimate=pl.CostEstimate(flops=24 << 30, bytes_accessed=4 << 20, transcendentals=1 << 24),
        name="soft_kmeans",
    )(embeddings, cluster_ids.reshape(32, 128), own)
    shapes = (jax.ShapeDtypeStruct((OWN, D), F32), jax.ShapeDtypeStruct((1, OWN), F32))
    out, mass = pl.pallas_call(
        deliver,
        out_shape=shapes,
        in_specs=[pl.BlockSpec(memory_space=pltpu.VMEM)] * 2,
        out_specs=(pl.BlockSpec(memory_space=pltpu.VMEM),) * 2,
        name="deliver",
    )(out, mass)
    return out[None], mass


def solution(mesh):
    placed = (P(("group", "member"), None), P(("group", "member")), P("group", "member", None))
    return jax.shard_map(
        local,
        mesh=mesh,
        in_specs=placed,
        out_specs=(P("group", "member", None), P("group", "member")),
        check_vma=False,
    )
```

```python
import functools
import math

import jax
import jax.numpy as jnp
from jax import lax
from jax.experimental import pallas as pl
from jax.experimental.pallas import tpu as pltpu
from jax.sharding import PartitionSpec as P

F32, BF16 = jnp.float32, jnp.bfloat16
MESH = pl.DeviceIdType.MESH
NT = (((1,), (1,)), ((), ()))
LOG2E = 1.4426950408889634
PRIOR_MASS = 1.0

SIDE = 4
CLUSTERS = 16
D = 256
ROWS = 4096
BLOCK = 256
BLOCKS = 32
STEP_OF = (0, 1, 3, 4, 12, 2, 8, 5, 15, 7, 13, 6, 14, 9, 11, 10)
VISITS = 8
GROUPS = ((0, 16), (16, 12), (28, 4))
CHUNK = 256
CHUNKS = 8
OWN = 512
STEPS = 8
LEVELS = 32767.0


def iota(shape, dim):
    return lax.broadcasted_iota(jnp.int32, shape, dim)


def ranks(ids, r_ref):
    upper = (iota((128, 128), 0) <= iota((128, 128), 1)).astype(F32).astype(BF16)
    ones = jnp.ones((128, 128), BF16)
    ri, ci = iota((128, 128), 0), iota((128, 128), 1)
    before = ((ri // 32 == ci // 32) & (ci < ri)).astype(F32).astype(BF16)
    for quad in range(CLUSTERS // 4):
        eq = jnp.concatenate(
            [(ids == quad * 4 + i).astype(F32) for i in range(4)], axis=0
        )
        hot = eq.astype(BF16)
        inside = jnp.dot(hot, upper, preferred_element_type=F32)
        totals = jnp.dot(hot, ones, preferred_element_type=F32).astype(BF16)
        ahead = jnp.dot(before, totals, preferred_element_type=F32)
        rank = jnp.where(eq > 0.5, inside + ahead - 1.0, -1.0)
        for i in range(4):
            r_ref[quad * 4 + i] = rank[i * 32 : (i + 1) * 32]


def permuted(clusters, r_ref, embt_ref):
    place = iota((BLOCK, 128), 0).astype(F32).astype(BF16)
    one, zero = jnp.ones_like(place), jnp.zeros_like(place)
    both = []
    for cluster in clusters:
        rank = r_ref[cluster]
        hots = []
        for t in range(ROWS // 128):
            row = jnp.broadcast_to(rank[t : t + 1], (BLOCK, 128)).astype(BF16)
            hots.append(jnp.where(row == place, one, zero))
        both.append(jnp.concatenate(hots, axis=1))
    hot = jnp.concatenate(both, axis=0)
    out = lax.dot_general(embt_ref[...], hot, NT, preferred_element_type=F32)
    return out.astype(BF16)


def visits():
    rounds = [(0, 1, 2, 3)]
    rounds += [(2 * i + 2, 2 * i + 3, 2 * i + 14, 2 * i + 15) for i in range(1, 7)]
    return rounds + [(28, 29, 30, 31)]


def kernel(emb_hbm, ids_ref, cent_ref, out_ref, mass_ref,
           emb_ref, embt_ref, send_ref, xt_ref, r_ref, cbuf_ref, bias_ref, e_ref,
           m_ref, s_ref, stat_ref, peer_ref, f_ref, acc_ref, qs_ref, qr_ref, ss_ref, sr_ref,
           row_s, row_r, cent_s, cent_r, fwd_s, fwd_r, stat_s, stat_r,
           sum_s, sum_r, side_s, side_r, emb_s):
    g, m = lax.axis_index("group"), lax.axis_index("member")
    y, x = g // SIDE, g % SIDE
    z, core = m // 2, m % 2
    partner = (g, z * 2 + 1 - core)

    def plane(j):
        o = sum(jnp.where(j == k, STEP_OF[k], 0) for k in range(CLUSTERS))
        return ((y + o // SIDE) % SIDE) * SIDE + (x + o % SIDE) % SIDE

    def column(dz):
        return (g, ((z + dz) % SIDE) * 2 + core)

    def row_copy(j):
        return pltpu.make_async_remote_copy(
            src_ref=send_ref.at[j], dst_ref=xt_ref.at[j], send_sem=row_s.at[j],
            recv_sem=row_r.at[j], device_id=(plane(j), m), device_id_type=MESH)

    def cent_copy(dz):
        return pltpu.make_async_remote_copy(
            src_ref=cent_ref, dst_ref=cbuf_ref.at[z], send_sem=cent_s.at[dz],
            recv_sem=cent_r.at[dz], device_id=column(dz), device_id_type=MESH)

    def fwd_copy(j):
        return pltpu.make_async_remote_copy(
            src_ref=xt_ref.at[j], dst_ref=xt_ref.at[CLUSTERS + j], send_sem=fwd_s.at[j],
            recv_sem=fwd_r.at[j], device_id=partner, device_id_type=MESH)

    def stat_copy(group):
        start, size = GROUPS[group]
        return pltpu.make_async_remote_copy(
            src_ref=stat_ref.at[pl.ds(start, size)],
            dst_ref=peer_ref.at[pl.ds((start + CLUSTERS) % BLOCKS, size)],
            send_sem=stat_s.at[group], recv_sem=stat_r.at[group],
            device_id=partner, device_id_type=MESH)

    def sum_copy(u):
        return pltpu.make_async_remote_copy(
            src_ref=qs_ref.at[u], dst_ref=qr_ref.at[u], send_sem=sum_s.at[u],
            recv_sem=sum_r.at[u], device_id=column(1 + 2 * (u % 2)), device_id_type=MESH)

    def side_copy(u):
        return pltpu.make_async_remote_copy(
            src_ref=ss_ref.at[u], dst_ref=sr_ref.at[u], send_sem=side_s.at[u],
            recv_sem=side_r.at[u], device_id=column(1 + 2 * (u % 2)), device_id_type=MESH)

    load = pltpu.make_async_copy(emb_hbm, emb_ref, emb_s)
    load.start()
    barrier = pltpu.get_barrier_semaphore()

    @pl.loop(1, CLUSTERS)
    def _(j):
        pl.semaphore_signal(barrier, inc=1, device_id=(plane(j), m), device_id_type=MESH)

    for dz in range(1, SIDE):
        pl.semaphore_signal(barrier, inc=1, device_id=column(dz), device_id_type=MESH)
    pl.semaphore_signal(barrier, inc=1, device_id=partner, device_id_type=MESH)

    ranks(ids_ref[...], r_ref)
    load.wait()

    @pl.loop(0, ROWS // 512)
    def _(i):
        part = pl.ds(pl.multiple_of(i * 512, 512), 512)
        embt_ref[:, part] = emb_ref[part, :].T

    pl.semaphore_wait(barrier, CLUSTERS - 1 + SIDE - 1 + 1)

    for dz in range(1, SIDE):
        cent_copy(dz).start()
    cbuf_ref[z] = cent_ref[...]

    @pl.loop(0, CLUSTERS // 2)
    def _(i):
        j = 2 * i + 1
        pair = permuted((plane(j), plane((j + 1) % CLUSTERS)), r_ref, embt_ref)
        send_ref[j] = pair[:, :BLOCK]
        row_copy(j).start()

        @pl.when(j < CLUSTERS - 1)
        def _():
            send_ref[j + 1] = pair[:, BLOCK:]
            row_copy(j + 1).start()

        @pl.when(j == CLUSTERS - 1)
        def _():
            xt_ref[0] = pair[:, BLOCK:]

    fwd_copy(0).start()

    for dz in range(1, SIDE):
        cent_copy(dz).wait_recv()
    ones = jnp.ones((D, 128), BF16)

    @pl.loop(0, SIDE)
    def _(zz):
        c = cbuf_ref[zz].astype(F32)
        square = c * c
        high = square.astype(BF16)
        low = (square - high.astype(F32)).astype(BF16)
        norm = (jnp.dot(high, ones, preferred_element_type=F32)
                + jnp.dot(low, ones, preferred_element_type=F32))
        bias_ref[pl.ds(pl.multiple_of(zz * OWN, OWN), OWN)] = norm * (-LOG2E / math.sqrt(D))

    def combine(group):
        start, size = GROUPS[group]
        slots = slice(start, start + size)
        tops, sums = m_ref[slots], s_ref[slots]
        top = jnp.max(tops, axis=1, keepdims=True)
        total = jnp.sum(sums * jnp.exp2(tops - top), axis=1, keepdims=True)
        stat_ref[slots] = jnp.concatenate([top] * 4 + [total] * 4, axis=1)
        stat_copy(group).start()

    @pl.loop(0, VISITS)
    def _(i):
        first, last = i == 0, i == VISITS - 1
        one = jnp.where(first, 0, jnp.where(last, 28, 2 * i + 2))
        two = jnp.where(first, 2, jnp.where(last, 30, 2 * i + 14))
        slots = (one, one + 1, two, two + 1)

        @pl.when(first)
        def _():
            row_copy(1).wait_recv()
            fwd_copy(1).start()

        @pl.when(jnp.logical_not(last))
        def _():
            for k in range(2):
                row_copy(2 * i + 2 + k).wait_recv()
                fwd_copy(2 * i + 2 + k).start()

        @pl.when(i > 0)
        def _():
            for k in range(2):
                fwd_copy(2 * i - 2 + k).wait_recv()

        @pl.when(last)
        def _():
            for k in range(2):
                fwd_copy(CLUSTERS - 2 + k).wait_recv()
            combine(0)
            combine(1)

        xb = jnp.concatenate([xt_ref[slot] for slot in slots], axis=1)
        columns = pl.ds(pl.multiple_of(i * 4 * BLOCK, 4 * BLOCK), 4 * BLOCK)
        tops, sums = [], []
        for kc in range(CHUNKS):
            c = cbuf_ref[kc // 2, (kc % 2) * CHUNK : (kc % 2 + 1) * CHUNK, :]
            bias = bias_ref[kc * CHUNK : (kc + 1) * CHUNK]
            score = jnp.dot(c, xb, preferred_element_type=F32)
            logit = score * (2.0 * LOG2E / math.sqrt(D)) + jnp.concatenate([bias] * 8, axis=1)
            top = jnp.max(logit, axis=0, keepdims=True)
            e = jnp.exp2(logit - top)
            e_ref[kc, :, columns] = e.astype(BF16)
            tops.append(top)
            sums.append(jnp.sum(e, axis=0, keepdims=True))
        tops = jnp.concatenate(tops, axis=0)
        sums = jnp.concatenate(sums, axis=0)
        for k, slot in enumerate(slots):
            m_ref[slot] = tops[:, k * BLOCK : (k + 1) * BLOCK]
            s_ref[slot] = sums[:, k * BLOCK : (k + 1) * BLOCK]

    def factors(start, stop):
        slots = slice(start, stop)
        mine, theirs = stat_ref[slots], peer_ref[slots]
        top = jnp.maximum(mine[:, 0:1], theirs[:, 0:1])
        total = (mine[:, 4:5] * jnp.exp2(mine[:, 0:1] - top)
                 + theirs[:, 4:5] * jnp.exp2(theirs[:, 0:1] - top))
        f_ref[slots] = jnp.exp2(m_ref[slots] - top) * (1.0 / total)

    combine(2)
    for group in range(2):
        stat_copy(group).wait_recv()
    factors(0, GROUPS[1][1])
    factors(CLUSTERS, BLOCKS)
    stat_copy(2).wait_recv()
    factors(GROUPS[1][1], CLUSTERS)

    order = [slot for four in visits() for slot in four]

    def weighted(kc, acc):
        parts = []
        for slot in order:
            f = f_ref[slot, pl.ds(kc, 1), :]
            high = f.astype(BF16).astype(F32)
            rows = xt_ref[slot].astype(F32) * f
            rest = jnp.concatenate([high, f - high, jnp.zeros((14, BLOCK), F32)], axis=0)
            parts.append(jnp.concatenate([rows, rest], axis=0).astype(BF16))
        lhs = jnp.concatenate(parts, axis=1)
        acc[...] = lax.dot_general(lhs, e_ref[kc], NT, preferred_element_type=F32)

    def absorb(acc, slot):
        side_copy(slot).wait_recv()
        sum_copy(slot).wait_recv()
        side = sr_ref[slot]
        acc[0:D] += qr_ref[slot].astype(jnp.int32).astype(F32) * side[0:1]
        acc[D : D + 8] += jnp.broadcast_to(side[4:5], (8, CHUNK))

    @pl.loop(0, STEPS)
    def _(u):
        pair, odd = u // 2, u % 2
        hops = jnp.where(pair == 0, 2, jnp.where(pair == 3, 0, 1 + 2 * odd))
        part = jnp.where(pair == 1, 1 - odd, odd)
        acc = acc_ref.at[odd]
        weighted(((z + hops) % SIDE) * 2 + part, acc)
        mass = acc[D : D + 1] + acc[D + 1 : D + 2]
        acc[D : D + 8] = jnp.broadcast_to(mass, (8, CHUNK))

        @pl.when(pair == 2)
        def _():
            absorb(acc, u - 4)

        @pl.when(pair < 3)
        def _():
            w = acc[0:D]
            peak = jnp.maximum(jnp.max(jnp.abs(w), axis=0, keepdims=True), 1e-30)
            q = jnp.round(w * (LEVELS / peak)).astype(jnp.int32)
            qs_ref[u] = q.astype(jnp.int16)
            sum_copy(u).start()
            ss_ref[u, 0:4] = jnp.broadcast_to(peak * (1.0 / LEVELS), (4, CHUNK))
            ss_ref[u, 4:8] = acc[D : D + 4]
            side_copy(u).start()

    @pl.loop(0, 2)
    def _(part):
        acc = acc_ref.at[part]
        absorb(acc, 3 - part)
        absorb(acc, 4 + part)
        rows = pl.ds(pl.multiple_of(part * CHUNK, CHUNK), CHUNK)
        total = acc[D : D + 1]
        mass_ref[:, rows] = total
        den = jnp.broadcast_to(total + PRIOR_MASS, (128, CHUNK)).T
        den = jnp.concatenate([den, den], axis=1)
        prior = PRIOR_MASS * cent_ref[rows, :].astype(F32)
        out_ref[rows, :] = (acc[0:D].T + prior) / den

    @pl.loop(0, STEPS - 2)
    def _(u):
        side_copy(u).wait_send()
        sum_copy(u).wait_send()

    for dz in range(1, SIDE):
        cent_copy(dz).wait_send()
    for group in range(3):
        stat_copy(group).wait_send()
    fwd_copy(0).wait_send()

    @pl.loop(1, CLUSTERS)
    def _(j):
        row_copy(j).wait_send()
        fwd_copy(j).wait_send()


def local(embeddings, cluster_ids, centroids):
    dma = pltpu.SemaphoreType.DMA
    own = centroids[0]
    out, mass = pl.pallas_call(
        kernel,
        out_shape=(pltpu.VMEM((OWN, D), F32), pltpu.VMEM((1, OWN), F32)),
        in_specs=[pl.BlockSpec(memory_space=pl.ANY)] + [pl.BlockSpec(memory_space=pltpu.VMEM)] * 2,
        out_specs=(pl.BlockSpec(memory_space=pltpu.VMEM),) * 2,
        scratch_shapes=[
            pltpu.VMEM((ROWS, D), BF16),
            pltpu.VMEM((D, ROWS), BF16),
            pltpu.VMEM((CLUSTERS, D, BLOCK), BF16),
            pltpu.VMEM((BLOCKS, D, BLOCK), BF16),
            pltpu.VMEM((CLUSTERS, 32, 128), F32),
            pltpu.VMEM((SIDE, OWN, D), BF16),
            pltpu.VMEM((SIDE * OWN, 128), F32),
            pltpu.VMEM((CHUNKS, CHUNK, BLOCKS * BLOCK), BF16),
            pltpu.VMEM((BLOCKS, CHUNKS, BLOCK), F32),
            pltpu.VMEM((BLOCKS, CHUNKS, BLOCK), F32),
            pltpu.VMEM((BLOCKS, 8, BLOCK), F32),
            pltpu.VMEM((BLOCKS, 8, BLOCK), F32),
            pltpu.VMEM((BLOCKS, CHUNKS, BLOCK), F32),
            pltpu.VMEM((2, D + 16, CHUNK), F32),
            pltpu.VMEM((STEPS - 2, D, CHUNK), jnp.int16),
            pltpu.VMEM((STEPS - 2, D, CHUNK), jnp.int16),
            pltpu.VMEM((STEPS - 2, 8, CHUNK), F32),
            pltpu.VMEM((STEPS - 2, 8, CHUNK), F32),
            dma((CLUSTERS,)), dma((CLUSTERS,)), dma((SIDE,)), dma((SIDE,)),
            dma((CLUSTERS,)), dma((CLUSTERS,)), dma((3,)), dma((3,)),
            dma((STEPS - 2,)), dma((STEPS - 2,)), dma((STEPS - 2,)), dma((STEPS - 2,)), dma,
        ],
        compiler_params=pltpu.CompilerParams(
            collective_id=0, has_side_effects=True, vmem_limit_bytes=57 << 20),
        cost_estimate=pl.CostEstimate(flops=24 << 30, bytes_accessed=4 << 20, transcendentals=1 << 24),
        name="soft_kmeans",
    )(embeddings, cluster_ids.reshape(32, 128), own)
    return out[None], mass


def solution(mesh):
    placed = (P(("group", "member"), None), P(("group", "member")), P("group", "member", None))
    return jax.shard_map(
        local,
        mesh=mesh,
        in_specs=placed,
        out_specs=(P("group", "member", None), P("group", "member")),
        check_vma=False,
    )
```

```python
import functools
import math

import jax
import jax.numpy as jnp
from jax import lax
from jax.experimental import pallas as pl
from jax.experimental.pallas import tpu as pltpu
from jax.sharding import PartitionSpec as P

F32, BF16 = jnp.float32, jnp.bfloat16
MESH = pl.DeviceIdType.MESH
NT = (((1,), (1,)), ((), ()))
LOG2E = 1.4426950408889634
PRIOR_MASS = 1.0

SIDE = 4
CLUSTERS = 16
D = 256
ROWS = 4096
BLOCK = 256
BLOCKS = 32
STEP_OF = (0, 1, 3, 4, 12, 2, 8, 5, 15, 7, 13, 6, 14, 9, 11, 10)
VISITS = 8
GROUPS = ((0, 16), (16, 12), (28, 4))
CHUNK = 256
CHUNKS = 8
OWN = 512
STEPS = 8
LEVELS = 32767.0


def iota(shape, dim):
    return lax.broadcasted_iota(jnp.int32, shape, dim)


def ranks(ids, r_ref):
    upper = (iota((128, 128), 0) <= iota((128, 128), 1)).astype(F32).astype(BF16)
    ones = jnp.ones((128, 128), BF16)
    ri, ci = iota((128, 128), 0), iota((128, 128), 1)
    before = ((ri // 32 == ci // 32) & (ci < ri)).astype(F32).astype(BF16)
    for quad in range(CLUSTERS // 4):
        eq = jnp.concatenate(
            [(ids == quad * 4 + i).astype(F32) for i in range(4)], axis=0
        )
        hot = eq.astype(BF16)
        inside = jnp.dot(hot, upper, preferred_element_type=F32)
        totals = jnp.dot(hot, ones, preferred_element_type=F32).astype(BF16)
        ahead = jnp.dot(before, totals, preferred_element_type=F32)
        rank = jnp.where(eq > 0.5, inside + ahead - 1.0, -1.0)
        for i in range(4):
            r_ref[quad * 4 + i] = rank[i * 32 : (i + 1) * 32]


def permuted(clusters, r_ref, embt_ref):
    place = iota((BLOCK, 128), 0).astype(F32).astype(BF16)
    one, zero = jnp.ones_like(place), jnp.zeros_like(place)
    both = []
    for cluster in clusters:
        rank = r_ref[cluster]
        hots = []
        for t in range(ROWS // 128):
            row = jnp.broadcast_to(rank[t : t + 1], (BLOCK, 128)).astype(BF16)
            hots.append(jnp.where(row == place, one, zero))
        both.append(jnp.concatenate(hots, axis=1))
    hot = jnp.concatenate(both, axis=0)
    out = lax.dot_general(embt_ref[...], hot, NT, preferred_element_type=F32)
    return out.astype(BF16)


def visits():
    rounds = [(0, 1, 2, 3)]
    rounds += [(2 * i + 2, 2 * i + 3, 2 * i + 14, 2 * i + 15) for i in range(1, 7)]
    return rounds + [(28, 29, 30, 31)]


def kernel(emb_hbm, ids_ref, cent_ref, out_ref, mass_ref,
           emb_ref, embt_ref, send_ref, xt_ref, r_ref, cbuf_ref, bias_ref, e_ref,
           m_ref, s_ref, stat_ref, peer_ref, f_ref, acc_ref, qs_ref, qr_ref, ss_ref, sr_ref,
           row_s, row_r, cent_s, cent_r, fwd_s, fwd_r, stat_s, stat_r,
           sum_s, sum_r, side_s, side_r, emb_s):
    g, m = lax.axis_index("group"), lax.axis_index("member")
    y, x = g // SIDE, g % SIDE
    z, core = m // 2, m % 2
    partner = (g, z * 2 + 1 - core)

    def plane(j):
        o = sum(jnp.where(j == k, STEP_OF[k], 0) for k in range(CLUSTERS))
        return ((y + o // SIDE) % SIDE) * SIDE + (x + o % SIDE) % SIDE

    def column(dz):
        return (g, ((z + dz) % SIDE) * 2 + core)

    def row_copy(j):
        return pltpu.make_async_remote_copy(
            src_ref=send_ref.at[j], dst_ref=xt_ref.at[j], send_sem=row_s.at[j],
            recv_sem=row_r.at[j], device_id=(plane(j), m), device_id_type=MESH)

    def cent_copy(dz):
        return pltpu.make_async_remote_copy(
            src_ref=cent_ref, dst_ref=cbuf_ref.at[z], send_sem=cent_s.at[dz],
            recv_sem=cent_r.at[dz], device_id=column(dz), device_id_type=MESH)

    def fwd_copy(j):
        return pltpu.make_async_remote_copy(
            src_ref=xt_ref.at[j], dst_ref=xt_ref.at[CLUSTERS + j], send_sem=fwd_s.at[j],
            recv_sem=fwd_r.at[j], device_id=partner, device_id_type=MESH)

    def stat_copy(group):
        start, size = GROUPS[group]
        return pltpu.make_async_remote_copy(
            src_ref=stat_ref.at[pl.ds(start, size)],
            dst_ref=peer_ref.at[pl.ds((start + CLUSTERS) % BLOCKS, size)],
            send_sem=stat_s.at[group], recv_sem=stat_r.at[group],
            device_id=partner, device_id_type=MESH)

    def sum_copy(u):
        return pltpu.make_async_remote_copy(
            src_ref=qs_ref.at[u], dst_ref=qr_ref.at[u], send_sem=sum_s.at[u],
            recv_sem=sum_r.at[u], device_id=column(1 + 2 * (u % 2)), device_id_type=MESH)

    def side_copy(u):
        return pltpu.make_async_remote_copy(
            src_ref=ss_ref.at[u], dst_ref=sr_ref.at[u], send_sem=side_s.at[u],
            recv_sem=side_r.at[u], device_id=column(1 + 2 * (u % 2)), device_id_type=MESH)

    load = pltpu.make_async_copy(emb_hbm, emb_ref, emb_s)
    load.start()
    barrier = pltpu.get_barrier_semaphore()

    @pl.loop(1, CLUSTERS)
    def _(j):
        pl.semaphore_signal(barrier, inc=1, device_id=(plane(j), m), device_id_type=MESH)

    for dz in range(1, SIDE):
        pl.semaphore_signal(barrier, inc=1, device_id=column(dz), device_id_type=MESH)
    pl.semaphore_signal(barrier, inc=1, device_id=partner, device_id_type=MESH)

    ranks(ids_ref[...], r_ref)
    load.wait()

    @pl.loop(0, ROWS // 512)
    def _(i):
        part = pl.ds(pl.multiple_of(i * 512, 512), 512)
        embt_ref[:, part] = emb_ref[part, :].T

    pl.semaphore_wait(barrier, CLUSTERS - 1 + SIDE - 1 + 1)

    for dz in range(1, SIDE):
        cent_copy(dz).start()
    cbuf_ref[z] = cent_ref[...]

    @pl.loop(0, CLUSTERS // 2)
    def _(i):
        j = 2 * i + 1
        pair = permuted((plane(j), plane((j + 1) % CLUSTERS)), r_ref, embt_ref)
        send_ref[j] = pair[:, :BLOCK]
        row_copy(j).start()

        @pl.when(j < CLUSTERS - 1)
        def _():
            send_ref[j + 1] = pair[:, BLOCK:]
            row_copy(j + 1).start()

        @pl.when(j == CLUSTERS - 1)
        def _():
            xt_ref[0] = pair[:, BLOCK:]

    fwd_copy(0).start()

    for dz in range(1, SIDE):
        cent_copy(dz).wait_recv()
    ones = jnp.ones((D, 128), BF16)

    @pl.loop(0, SIDE)
    def _(zz):
        c = cbuf_ref[zz].astype(F32)
        square = c * c
        high = square.astype(BF16)
        low = (square - high.astype(F32)).astype(BF16)
        norm = (jnp.dot(high, ones, preferred_element_type=F32)
                + jnp.dot(low, ones, preferred_element_type=F32))
        bias_ref[pl.ds(pl.multiple_of(zz * OWN, OWN), OWN)] = norm * (-LOG2E / math.sqrt(D))

    def combine(group):
        start, size = GROUPS[group]
        slots = slice(start, start + size)
        tops, sums = m_ref[slots], s_ref[slots]
        top = jnp.max(tops, axis=1, keepdims=True)
        total = jnp.sum(sums * jnp.exp2(tops - top), axis=1, keepdims=True)
        stat_ref[slots] = jnp.concatenate([top] * 4 + [total] * 4, axis=1)
        stat_copy(group).start()

    @pl.loop(0, VISITS)
    def _(i):
        first, last = i == 0, i == VISITS - 1
        one = jnp.where(first, 0, jnp.where(last, 28, 2 * i + 2))
        two = jnp.where(first, 2, jnp.where(last, 30, 2 * i + 14))
        slots = (one, one + 1, two, two + 1)

        @pl.when(first)
        def _():
            row_copy(1).wait_recv()
            fwd_copy(1).start()

        @pl.when(jnp.logical_not(last))
        def _():
            for k in range(2):
                row_copy(2 * i + 2 + k).wait_recv()
                fwd_copy(2 * i + 2 + k).start()

        @pl.when(i > 0)
        def _():
            for k in range(2):
                fwd_copy(2 * i - 2 + k).wait_recv()

        @pl.when(last)
        def _():
            for k in range(2):
                fwd_copy(CLUSTERS - 2 + k).wait_recv()
            combine(0)
            combine(1)

        xb = jnp.concatenate([xt_ref[slot] for slot in slots], axis=1)
        columns = pl.ds(pl.multiple_of(i * 4 * BLOCK, 4 * BLOCK), 4 * BLOCK)
        tops, sums = [], []
        for kc in range(CHUNKS):
            c = cbuf_ref[kc // 2, (kc % 2) * CHUNK : (kc % 2 + 1) * CHUNK, :]
            bias = bias_ref[kc * CHUNK : (kc + 1) * CHUNK]
            score = jnp.dot(c, xb, preferred_element_type=F32)
            logit = score * (2.0 * LOG2E / math.sqrt(D)) + jnp.concatenate([bias] * 8, axis=1)
            top = jnp.max(logit, axis=0, keepdims=True)
            e = jnp.exp2(logit - top)
            e_ref[kc, :, columns] = e.astype(BF16)
            tops.append(top)
            sums.append(jnp.sum(e, axis=0, keepdims=True))
        tops = jnp.concatenate(tops, axis=0)
        sums = jnp.concatenate(sums, axis=0)
        for k, slot in enumerate(slots):
            m_ref[slot] = tops[:, k * BLOCK : (k + 1) * BLOCK]
            s_ref[slot] = sums[:, k * BLOCK : (k + 1) * BLOCK]

    def factors(start, stop):
        slots = slice(start, stop)
        mine, theirs = stat_ref[slots], peer_ref[slots]
        top = jnp.maximum(mine[:, 0:1], theirs[:, 0:1])
        total = (mine[:, 4:5] * jnp.exp2(mine[:, 0:1] - top)
                 + theirs[:, 4:5] * jnp.exp2(theirs[:, 0:1] - top))
        f_ref[slots] = jnp.exp2(m_ref[slots] - top) * (1.0 / total)

    combine(2)
    for group in range(2):
        stat_copy(group).wait_recv()
    factors(0, GROUPS[1][1])
    factors(CLUSTERS, BLOCKS)
    stat_copy(2).wait_recv()
    factors(GROUPS[1][1], CLUSTERS)

    order = [slot for four in visits() for slot in four]

    def weighted(kc, acc):
        parts = []
        for slot in order:
            f = f_ref[slot, pl.ds(kc, 1), :]
            high = f.astype(BF16).astype(F32)
            rows = xt_ref[slot].astype(F32) * f
            rest = jnp.concatenate([high, f - high, jnp.zeros((14, BLOCK), F32)], axis=0)
            parts.append(jnp.concatenate([rows, rest], axis=0).astype(BF16))
        lhs = jnp.concatenate(parts, axis=1)
        acc[...] = lax.dot_general(lhs, e_ref[kc], NT, preferred_element_type=F32)

    def absorb(acc, slot):
        side_copy(slot).wait_recv()
        sum_copy(slot).wait_recv()
        side = sr_ref[slot]
        acc[0:D] += qr_ref[slot].astype(jnp.int32).astype(F32) * side[0:1]
        acc[D : D + 8] += jnp.broadcast_to(side[4:5], (8, CHUNK))

    @pl.loop(0, STEPS)
    def _(u):
        pair, odd = u // 2, u % 2
        hops = jnp.where(pair == 0, 2, jnp.where(pair == 3, 0, 1 + 2 * odd))
        part = jnp.where(pair == 1, 1 - odd, odd)
        acc = acc_ref.at[odd]
        weighted(((z + hops) % SIDE) * 2 + part, acc)
        mass = acc[D : D + 1] + acc[D + 1 : D + 2]
        acc[D : D + 8] = jnp.broadcast_to(mass, (8, CHUNK))

        @pl.when(pair == 2)
        def _():
            absorb(acc, u - 4)

        @pl.when(pair < 3)
        def _():
            w = acc[0:D]
            peak = jnp.maximum(jnp.max(jnp.abs(w), axis=0, keepdims=True), 1e-30)
            q = jnp.round(w * (LEVELS / peak)).astype(jnp.int32)
            qs_ref[u] = q.astype(jnp.int16)
            sum_copy(u).start()
            ss_ref[u, 0:4] = jnp.broadcast_to(peak * (1.0 / LEVELS), (4, CHUNK))
            ss_ref[u, 4:8] = acc[D : D + 4]
            side_copy(u).start()

    for dz in range(1, SIDE):
        cent_copy(dz).wait_send()
    for group in range(3):
        stat_copy(group).wait_send()
    fwd_copy(0).wait_send()

    @pl.loop(1, CLUSTERS)
    def _(j):
        row_copy(j).wait_send()
        fwd_copy(j).wait_send()

    @pl.loop(0, 2)
    def _(part):
        acc = acc_ref.at[part]
        absorb(acc, 3 - part)
        absorb(acc, 4 + part)
        rows = pl.ds(pl.multiple_of(part * CHUNK, CHUNK), CHUNK)
        total = acc[D : D + 1]
        mass_ref[:, rows] = total
        den = jnp.broadcast_to(total + PRIOR_MASS, (128, CHUNK)).T
        den = jnp.concatenate([den, den], axis=1)
        prior = PRIOR_MASS * cent_ref[rows, :].astype(F32)
        out_ref[rows, :] = (acc[0:D].T + prior) / den

    @pl.loop(0, STEPS - 2)
    def _(u):
        side_copy(u).wait_send()
        sum_copy(u).wait_send()


def local(embeddings, cluster_ids, centroids):
    dma = pltpu.SemaphoreType.DMA
    own = centroids[0]
    out, mass = pl.pallas_call(
        kernel,
        out_shape=(pltpu.VMEM((OWN, D), F32), pltpu.VMEM((1, OWN), F32)),
        in_specs=[pl.BlockSpec(memory_space=pl.ANY)] + [pl.BlockSpec(memory_space=pltpu.VMEM)] * 2,
        out_specs=(pl.BlockSpec(memory_space=pltpu.VMEM),) * 2,
        scratch_shapes=[
            pltpu.VMEM((ROWS, D), BF16),
            pltpu.VMEM((D, ROWS), BF16),
            pltpu.VMEM((CLUSTERS, D, BLOCK), BF16),
            pltpu.VMEM((BLOCKS, D, BLOCK), BF16),
            pltpu.VMEM((CLUSTERS, 32, 128), F32),
            pltpu.VMEM((SIDE, OWN, D), BF16),
            pltpu.VMEM((SIDE * OWN, 128), F32),
            pltpu.VMEM((CHUNKS, CHUNK, BLOCKS * BLOCK), BF16),
            pltpu.VMEM((BLOCKS, CHUNKS, BLOCK), F32),
            pltpu.VMEM((BLOCKS, CHUNKS, BLOCK), F32),
            pltpu.VMEM((BLOCKS, 8, BLOCK), F32),
            pltpu.VMEM((BLOCKS, 8, BLOCK), F32),
            pltpu.VMEM((BLOCKS, CHUNKS, BLOCK), F32),
            pltpu.VMEM((2, D + 16, CHUNK), F32),
            pltpu.VMEM((STEPS - 2, D, CHUNK), jnp.int16),
            pltpu.VMEM((STEPS - 2, D, CHUNK), jnp.int16),
            pltpu.VMEM((STEPS - 2, 8, CHUNK), F32),
            pltpu.VMEM((STEPS - 2, 8, CHUNK), F32),
            dma((CLUSTERS,)), dma((CLUSTERS,)), dma((SIDE,)), dma((SIDE,)),
            dma((CLUSTERS,)), dma((CLUSTERS,)), dma((3,)), dma((3,)),
            dma((STEPS - 2,)), dma((STEPS - 2,)), dma((STEPS - 2,)), dma((STEPS - 2,)), dma,
        ],
        compiler_params=pltpu.CompilerParams(
            collective_id=0, has_side_effects=True, vmem_limit_bytes=57 << 20),
        cost_estimate=pl.CostEstimate(flops=24 << 30, bytes_accessed=4 << 20, transcendentals=1 << 24),
        name="soft_kmeans",
    )(embeddings, cluster_ids.reshape(32, 128), own)
    return out[None], mass


def solution(mesh):
    placed = (P(("group", "member"), None), P(("group", "member")), P("group", "member", None))
    return jax.shard_map(
        local,
        mesh=mesh,
        in_specs=placed,
        out_specs=(P("group", "member", None), P("group", "member")),
        check_vma=False,
    )
```
